32 devices in a mesh: rep: 16 (over z, x, core), shard: 2 (over y).
Axes of the slice: x: 2, y: 2, z: 4, core: 2. Of those that a mesh axis runs over, the one named last changes fastest.
Arguments:
- tokens: bfloat16 [16384, 1024], P(('rep', 'shard')), may hold values from -6 to 6
- ln1_gain: bfloat16 [1024], P('shard'), may hold values from 0.25 to 1.75
- ln1_bias: bfloat16 [1024], P('shard'), may hold values from -1.5 to 1.5
- qkv_weight: bfloat16 [1024, 3072], P('shard'), may hold values from -0.1875 to 0.1875
- qv_bias: bfloat16 [2048], P('shard'), may hold values from -1.5 to 1.5
- proj_weight: bfloat16 [1024, 1024], P('shard'), may hold values from -0.5 to 0.5
- proj_bias: bfloat16 [1024], P('shard'), may hold values from -1.5 to 1.5
- ln2_gain: bfloat16 [1024], P('shard'), may hold values from 0.25 to 1.75
- ln2_bias: bfloat16 [1024], P('shard'), may hold values from -1.5 to 1.5
- fc1_weight: bfloat16 [1024, 4096], P('shard'), may hold values from -0.1875 to 0.1875
- fc1_bias: bfloat16 [4096], P('shard'), may hold values from -1.5 to 1.5
- fc2_weight: bfloat16 [4096, 1024], P('shard'), may hold values from -0.125 to 0.125
- fc2_bias: bfloat16 [1024], P('shard'), may hold values from -1.5 to 1.5
- cotangent: bfloat16 [16384, 1024], P(('rep', 'shard')), may hold values from -16 to 16
Outputs:
- layer_out: bfloat16 [16384, 1024], P(('rep', 'shard'))
- grad_tokens: float32 [16384, 1024], P(('rep', 'shard'))
- grad_ln1_gain: float32 [1024], P('shard')
- grad_ln1_bias: float32 [1024], P('shard')
- grad_qkv_weight: float32 [1024, 3072], P('shard')
- grad_qv_bias: float32 [2048], P('shard')
- grad_proj_weight: float32 [1024, 1024], P('shard')
- grad_proj_bias: float32 [1024], P('shard')
- grad_ln2_gain: float32 [1024], P('shard')
- grad_ln2_bias: float32 [1024], P('shard')
- grad_fc1_weight: float32 [1024, 4096], P('shard')
- grad_fc1_bias: float32 [4096], P('shard')
- grad_fc2_weight: float32 [4096, 1024], P('shard')
- grad_fc2_bias: float32 [1024], P('shard')
The draws below stay inside these ranges and needn't reach their ends.
All inputs are finite; a program needn't handle non-finite values.
Results may differ from the reference program's by a relative error of at most 0.018.
Values may be sent and summed in bfloat16 or wider, within the bound.
A program may use at most 320 MiB of HBM per device.

```python
import jax
import jax.numpy as jnp
from jax import lax

D = 1024
HEADS = 16
HEAD = 64
FF = 4096
SEQ = 1024
TOKENS = 16384


def draw_cotangent(key, part):
    key = jax.random.fold_in(key, 7)
    seq_count = TOKENS // SEQ
    place = (jnp.arange(TOKENS) // SEQ).astype(jnp.float32) / max(seq_count - 1, 1)
    base = jnp.clip(jax.random.normal(key, (TOKENS, D), jnp.float32), -4.0, 4.0)
    row_scale = 3.0 ** place
    return (base * row_scale[:, None]).astype(jnp.bfloat16)


def block_scale(own_key, shape, cuts, low, largest):
    def one(dim, blocks):
        steps = jax.random.uniform(jax.random.fold_in(jax.random.fold_in(own_key, 6), dim), (blocks,), jnp.float32, low / len(cuts), largest / len(cuts))
        return jnp.repeat(jnp.exp(steps), shape[dim] // blocks).reshape((-1,) + (1,) * (len(shape) - dim - 1))

    level = one(*cuts[0])
    for cut in cuts[1:]:
        level = level * one(*cut)
    return level


def bell_draw(stream_key, dims, deviation, limit, pieces=(), held_as=jnp.bfloat16):
    array = deviation * jax.random.normal(stream_key, dims, jnp.float32)
    if pieces:
        array = array * block_scale(stream_key, dims, pieces, -0.22, 0.18)
    return jnp.clip(array, -limit, limit).astype(held_as)


def setup_inputs(seed: int = 0) -> dict:
    arg_keys = jax.random.split(jax.random.key(seed), 15)
    return {
        "tokens": bell_draw(arg_keys[0], (TOKENS, D), 1.0, 6.0, ((0, 32),)),
        "ln1_gain": jnp.clip(1.0 + 0.15 * jax.random.normal(arg_keys[1], (D,), jnp.float32), 0.25, 1.75).astype(jnp.bfloat16),
        "ln1_bias": bell_draw(arg_keys[2], (D,), 0.3, 1.5, ((0, 2),)),
        "qkv_weight": bell_draw(arg_keys[3], (D, 3 * D), D ** -0.5, 0.1875, ((0, 2),)),
        "qv_bias": bell_draw(arg_keys[4], (2 * D,), 0.3, 1.5, ((0, 2),)),
        "proj_weight": bell_draw(arg_keys[5], (D, D), (D // 8) ** -0.5, 0.5, ((0, 2),)),
        "proj_bias": bell_draw(arg_keys[6], (D,), 0.3, 1.5, ((0, 2),)),
        "ln2_gain": jnp.clip(1.0 + 0.15 * jax.random.normal(arg_keys[7], (D,), jnp.float32), 0.25, 1.75).astype(jnp.bfloat16),
        "ln2_bias": bell_draw(arg_keys[8], (D,), 0.3, 1.5, ((0, 2),)),
        "fc1_weight": bell_draw(arg_keys[9], (D, FF), D ** -0.5, 0.1875, ((0, 2),)),
        "fc1_bias": bell_draw(arg_keys[10], (FF,), 0.3, 1.5, ((0, 2),)),
        "fc2_weight": bell_draw(arg_keys[11], (FF, D), (FF // 2) ** -0.5, 0.125, ((0, 2),)),
        "fc2_bias": bell_draw(arg_keys[12], (D,), 0.3, 1.5, ((0, 2),)),
        "cotangent": draw_cotangent(jax.random.fold_in(arg_keys[14], 71), 0),
    }


@jax.custom_vjp
def low(v):
    return lax.optimization_barrier(v.astype(jnp.bfloat16)).astype(jnp.float32)

@jax.custom_vjp
def low_back(v):
    return v

def low_keep(v):
    return (low(v), None)

def low_pass(kept, grad):
    return (grad,)

def back_keep(v):
    return (v, None)

def back_low(kept, grad):
    return (low(grad),)
low.defvjp(low_keep, low_pass)
low_back.defvjp(back_keep, back_low)

def layer_norm(values_in, gain_vec, shift_vec):
    centered = values_in - lax.optimization_barrier(jnp.mean(values_in, axis=-1, keepdims=True))
    inverse = lax.rsqrt(lax.optimization_barrier(jnp.mean(centered * centered, axis=-1, keepdims=True)) + 1e-05)
    return centered * inverse * gain_vec + shift_vec

def attend(queries, keys_all, values_all):
    seq_len = keys_all.shape[0]
    block_rows = min(512, seq_len)
    heads_count = queries.shape[1]
    slopes = 2.0 ** (-8.0 * (jnp.arange(heads_count) + 1.0) / heads_count)
    key_pos = jnp.arange(seq_len, dtype=jnp.int32)

    def one_block(first_row):
        query_rows = lax.dynamic_slice_in_dim(queries, first_row, block_rows, 0)
        scores = jnp.einsum('qhd,khd->hqk', query_rows, keys_all, precision=lax.Precision.HIGHEST) * HEAD ** (-0.5)
        scores = low_back(scores)
        query_pos = first_row + jnp.arange(block_rows, dtype=jnp.int32)
        distance = (query_pos[:, None] - key_pos[None, :]).astype(scores.dtype)
        scores = scores - slopes[:, None, None].astype(scores.dtype) * distance[None]
        causal = (key_pos[None, :] <= query_pos[:, None])[None]
        scores = jnp.where(causal, scores, -1e+30)
        attn_probs = low(jax.nn.softmax(scores, axis=-1))
        return jnp.einsum('hqk,khd->qhd', attn_probs, values_all, precision=lax.Precision.HIGHEST)
    starts = (jnp.arange(seq_len // block_rows) * block_rows).astype(jnp.int32)
    blocks_out = lax.map(jax.checkpoint(one_block), starts)
    return blocks_out.reshape(seq_len, heads_count * values_all.shape[2])

def layer(params, inputs):
    gain_one, shift_one, packed_weight, pair_bias, proj_weight, proj_bias, gain_two, shift_two, up_weight, up_bias, down_weight, down_bias = params
    normed_one = low(layer_norm(inputs, gain_one, shift_one))
    packed = jnp.dot(normed_one, packed_weight, precision=lax.Precision.HIGHEST)
    queries = low_back(low(packed[:, :D] + pair_bias[:D]))
    keys_all = low_back(low(packed[:, D:2 * D]))
    values_all = low_back(low(packed[:, 2 * D:] + pair_bias[D:]))
    mixed = attend(queries.reshape(-1, HEADS, HEAD), keys_all.reshape(-1, HEADS, HEAD), values_all.reshape(-1, HEADS, HEAD))
    mixed = low_back(low(mixed))
    resid = inputs + low_back(jnp.dot(mixed, proj_weight, precision=lax.Precision.HIGHEST) + proj_bias)
    normed_two = low(layer_norm(resid, gain_two, shift_two))
    hidden = low_back(jnp.dot(normed_two, up_weight, precision=lax.Precision.HIGHEST) + up_bias)
    active = low(jax.nn.gelu(hidden, approximate=True))
    return resid + jnp.dot(active, down_weight, precision=lax.Precision.HIGHEST) + down_bias

def reference(tokens, ln1_gain, ln1_bias, qkv_weight, qv_bias, proj_weight, proj_bias, ln2_gain, ln2_bias, fc1_weight, fc1_bias, fc2_weight, fc2_bias, cotangent):
    params = tuple((array_in.astype(jnp.float32) for array_in in (ln1_gain, ln1_bias, qkv_weight, qv_bias, proj_weight, proj_bias, ln2_gain, ln2_bias, fc1_weight, fc1_bias, fc2_weight, fc2_bias)))
    seq_count = tokens.shape[0] // SEQ
    inputs = tokens.astype(jnp.float32).reshape(seq_count, SEQ, D)
    cotan_seq = cotangent.astype(jnp.float32).reshape(seq_count, SEQ, D)

    def one_sequence(totals, seq_pair):
        outputs, backward = jax.vjp(layer, params, seq_pair[0])
        grad_parts, grad_in = backward(seq_pair[1])
        return (jax.tree.map(jnp.add, totals, grad_parts), (outputs, grad_in))
    zero_grads = jax.tree.map(jnp.zeros_like, params)
    totals, (outputs, grad_in) = lax.scan(one_sequence, zero_grads, (inputs, cotan_seq))
    return (outputs.reshape(-1, D).astype(jnp.bfloat16), grad_in.reshape(-1, D), totals[0], totals[1], totals[2], totals[3], totals[4], totals[5], totals[6], totals[7], totals[8], totals[9], totals[10], totals[11])
```

```python
import jax
import jax.numpy as jnp
from jax import lax
from jax.sharding import PartitionSpec as P

HEADS = 16
HEAD = 64


def normalize(values_in, gain_vec, shift_vec):
    centered = values_in - jnp.mean(values_in, axis=-1, keepdims=True)
    inverse = lax.rsqrt(jnp.mean(centered * centered, axis=-1, keepdims=True) + 1e-05)
    scaled = centered * inverse
    return (scaled * gain_vec + shift_vec, scaled, inverse)


def normal_back(grad_in, scaled, inverse, gain_vec):
    inner = grad_in * gain_vec
    return inverse * (
        inner
        - jnp.mean(inner, axis=-1, keepdims=True)
        - scaled * jnp.mean(inner * scaled, axis=-1, keepdims=True)
    )


def tanh_gelu(values_in):
    return jax.nn.gelu(values_in, approximate=True)


def owned_part(vector, pieces):
    length = vector.shape[0] // pieces
    return lax.dynamic_slice_in_dim(vector, lax.axis_index("shard") * length, length, 0)


def group_vectors(gain_sum, shift_sum):
    pieces = lax.axis_size("shard")
    summed_gain, summed_shift = lax.psum((gain_sum, shift_sum), "shard")
    return (owned_part(summed_gain, pieces), owned_part(summed_shift, pieces))


def score_block(query_heads, key_heads, first_row):
    tok_rows, heads_count, head_size = query_heads.shape
    seq_len = key_heads.shape[0]
    scores = jnp.einsum(
        "qhd,khd->hqk", query_heads, key_heads, preferred_element_type=jnp.float32
    ) * head_size ** (-0.5)
    slopes = 2.0 ** (-8.0 * (jnp.arange(heads_count, dtype=jnp.float32) + 1.0) / heads_count)
    query_pos = first_row + jnp.arange(tok_rows, dtype=jnp.int32)
    key_pos = jnp.arange(seq_len, dtype=jnp.int32)
    distance = (query_pos[:, None] - key_pos[None, :]).astype(jnp.float32)
    scores = scores - slopes[:, None, None] * distance[None]
    causal = (key_pos[None, :] <= query_pos[:, None])[None]
    return jnp.where(causal, scores, -1e30)


def per_device(
    tokens,
    ln1_gain,
    ln1_bias,
    qkv_weight,
    qv_bias,
    proj_weight,
    proj_bias,
    ln2_gain,
    ln2_bias,
    fc1_weight,
    fc1_bias,
    fc2_weight,
    fc2_bias,
    cotangent,
):
    f32 = jnp.float32
    bf16 = jnp.bfloat16
    tok_rows, width = tokens.shape
    pieces = lax.axis_size("shard")
    first_row = lax.axis_index("shard") * tok_rows
    gathered = (
        lax.all_gather(ln1_gain, "shard", axis=0, tiled=True),
        lax.all_gather(ln1_bias, "shard", axis=0, tiled=True),
        lax.all_gather(qkv_weight, "shard", axis=0, tiled=True),
        lax.all_gather(qv_bias, "shard", axis=0, tiled=True),
        lax.all_gather(proj_weight, "shard", axis=0, tiled=True),
        lax.all_gather(proj_bias, "shard", axis=0, tiled=True),
        lax.all_gather(ln2_gain, "shard", axis=0, tiled=True),
        lax.all_gather(ln2_bias, "shard", axis=0, tiled=True),
        lax.all_gather(fc1_weight, "shard", axis=0, tiled=True),
        lax.all_gather(fc1_bias, "shard", axis=0, tiled=True),
        lax.all_gather(fc2_weight, "shard", axis=0, tiled=True),
        lax.all_gather(fc2_bias, "shard", axis=0, tiled=True),
    )
    inputs = tokens.astype(f32)
    normed_one, scaled_one, inverse_one = normalize(
        inputs, gathered[0].astype(f32), gathered[1].astype(f32)
    )
    normed_one_b = normed_one.astype(bf16)
    packed = jnp.dot(normed_one_b, gathered[2], preferred_element_type=f32)
    pair_bias = gathered[3].astype(f32)
    query_b = (packed[:, :width] + pair_bias[:width]).astype(bf16)
    keys_b = packed[:, width : 2 * width].astype(bf16)
    values_b = (packed[:, 2 * width :] + pair_bias[width:]).astype(bf16)
    all_keys, all_values = (
        lax.all_gather(keys_b, "shard", axis=0, tiled=True),
        lax.all_gather(values_b, "shard", axis=0, tiled=True),
    )
    query_heads = query_b.reshape(tok_rows, HEADS, HEAD)
    key_heads = all_keys.reshape(-1, HEADS, HEAD)
    value_heads = all_values.reshape(-1, HEADS, HEAD)
    scores = score_block(query_heads, key_heads, first_row)
    row_max = jnp.max(scores, axis=-1, keepdims=True)
    exp_terms = jnp.exp(scores - row_max)
    row_total = jnp.sum(exp_terms, axis=-1, keepdims=True)
    logsum = row_max + jnp.log(row_total)
    probs_b = (exp_terms / row_total).astype(bf16)
    mixed_b = (
        jnp.einsum("hqk,khd->qhd", probs_b, value_heads, preferred_element_type=f32)
        .reshape(tok_rows, width)
        .astype(bf16)
    )
    resid = (
        inputs + jnp.dot(mixed_b, gathered[4], preferred_element_type=f32) + gathered[5].astype(f32)
    )
    normed_two, scaled_two, inverse_two = normalize(
        resid, gathered[6].astype(f32), gathered[7].astype(f32)
    )
    normed_two_b = normed_two.astype(bf16)
    hidden = jnp.dot(normed_two_b, gathered[8], preferred_element_type=f32) + gathered[9].astype(
        f32
    )
    active_b = tanh_gelu(hidden).astype(bf16)
    output = (
        resid
        + jnp.dot(active_b, gathered[10], preferred_element_type=f32)
        + gathered[11].astype(f32)
    )
    cotan = cotangent.astype(f32)
    grad_active = jnp.einsum("td,fd->tf", cotangent, gathered[10], preferred_element_type=f32)
    unused_value, gelu_back = jax.vjp(tanh_gelu, hidden)
    grad_hidden_b = gelu_back(grad_active)[0].astype(bf16)
    grad_norm_two = jnp.einsum("tf,df->td", grad_hidden_b, gathered[8], preferred_element_type=f32)
    grad_gain_two = jnp.sum(grad_norm_two * scaled_two, axis=0)
    grad_shift_two = jnp.sum(grad_norm_two, axis=0)
    grad_resid = cotan + normal_back(
        grad_norm_two, scaled_two, inverse_two, gathered[6].astype(f32)
    )
    owned_two, owned_active = (
        lax.all_to_all(normed_two_b, "shard", split_axis=1, concat_axis=0, tiled=True),
        lax.all_to_all(active_b, "shard", split_axis=1, concat_axis=0, tiled=True),
    )
    group_cotan, group_hidden = (
        lax.all_gather(cotangent, "shard", axis=0, tiled=True),
        lax.all_gather(grad_hidden_b, "shard", axis=0, tiled=True),
    )
    part_down = jnp.einsum("tf,td->fd", owned_active, group_cotan, preferred_element_type=f32)
    part_up = jnp.einsum("td,tf->df", owned_two, group_hidden, preferred_element_type=f32)
    part_down_bias = owned_part(jnp.sum(group_cotan.astype(f32), axis=0), pieces)
    part_up_bias = owned_part(jnp.sum(group_hidden.astype(f32), axis=0), pieces)
    part_gain_two, part_shift_two = group_vectors(grad_gain_two, grad_shift_two)
    grad_branch_b = grad_resid.astype(bf16)
    grad_mixed_b = jnp.einsum(
        "te,de->td", grad_branch_b, gathered[4], preferred_element_type=f32
    ).astype(bf16)
    grad_mixed_heads = grad_mixed_b.reshape(tok_rows, HEADS, HEAD)
    scores = score_block(query_heads, key_heads, first_row)
    attn_probs = jnp.exp(scores - logsum)
    probs_b = attn_probs.astype(bf16)
    grad_probs = jnp.einsum(
        "qhd,khd->hqk", grad_mixed_heads, value_heads, preferred_element_type=f32
    )
    row_delta = jnp.sum(attn_probs * grad_probs, axis=-1, keepdims=True)
    grad_scores_b = (attn_probs * (grad_probs - row_delta)).astype(bf16)
    score_scale = HEAD ** (-0.5)
    grad_query_b = (
        (
            jnp.einsum("hqk,khd->qhd", grad_scores_b, key_heads, preferred_element_type=f32)
            * score_scale
        )
        .reshape(tok_rows, width)
        .astype(bf16)
    )
    key_terms = (
        jnp.einsum("hqk,qhd->khd", grad_scores_b, query_heads, preferred_element_type=f32)
        * score_scale
    ).reshape(-1, width)
    value_terms = jnp.einsum(
        "hqk,qhd->khd", probs_b, grad_mixed_heads, preferred_element_type=f32
    ).reshape(-1, width)
    grad_keys, grad_values = (
        lax.psum_scatter(
            key_terms.astype(jnp.bfloat16), "shard", scatter_dimension=0, tiled=True
        ).astype(jnp.float32),
        lax.psum_scatter(
            value_terms.astype(jnp.bfloat16), "shard", scatter_dimension=0, tiled=True
        ).astype(jnp.float32),
    )
    grad_values_b = grad_values.astype(bf16)
    grad_packed_b = jnp.concatenate([grad_query_b, grad_keys.astype(bf16), grad_values_b], axis=1)
    grad_norm_one = jnp.einsum("te,de->td", grad_packed_b, gathered[2], preferred_element_type=f32)
    grad_gain_one = jnp.sum(grad_norm_one * scaled_one, axis=0)
    grad_shift_one = jnp.sum(grad_norm_one, axis=0)
    grad_inputs = grad_resid + normal_back(
        grad_norm_one, scaled_one, inverse_one, gathered[0].astype(f32)
    )
    owned_one, owned_mixed = (
        lax.all_to_all(normed_one_b, "shard", split_axis=1, concat_axis=0, tiled=True),
        lax.all_to_all(mixed_b, "shard", split_axis=1, concat_axis=0, tiled=True),
    )
    group_packed, group_branch = (
        lax.all_gather(grad_packed_b, "shard", axis=0, tiled=True),
        lax.all_gather(grad_branch_b, "shard", axis=0, tiled=True),
    )
    part_packed = jnp.einsum("td,te->de", owned_one, group_packed, preferred_element_type=f32)
    part_proj = jnp.einsum("td,te->de", owned_mixed, group_branch, preferred_element_type=f32)
    packed_sums = jnp.sum(group_packed.astype(f32), axis=0)
    part_pair = owned_part(jnp.concatenate([packed_sums[:width], packed_sums[2 * width :]]), pieces)
    part_proj_bias = owned_part(jnp.sum(group_branch.astype(f32), axis=0), pieces)
    part_gain_one, part_shift_one = group_vectors(grad_gain_one, grad_shift_one)
    (
        part_gain_one,
        part_shift_one,
        part_packed,
        part_pair,
        part_proj,
        part_proj_bias,
        part_gain_two,
        part_shift_two,
        part_up,
        part_up_bias,
        part_down,
        part_down_bias,
    ) = (
        lax.psum(part_gain_one.astype(jnp.bfloat16), "rep").astype(jnp.float32),
        lax.psum(part_shift_one.astype(jnp.bfloat16), "rep").astype(jnp.float32),
        lax.psum(part_packed.astype(jnp.bfloat16), "rep").astype(jnp.float32),
        lax.psum(part_pair.astype(jnp.bfloat16), "rep").astype(jnp.float32),
        lax.psum(part_proj.astype(jnp.bfloat16), "rep").astype(jnp.float32),
        lax.psum(part_proj_bias.astype(jnp.bfloat16), "rep").astype(jnp.float32),
        lax.psum(part_gain_two.astype(jnp.bfloat16), "rep").astype(jnp.float32),
        lax.psum(part_shift_two.astype(jnp.bfloat16), "rep").astype(jnp.float32),
        lax.psum(part_up.astype(jnp.bfloat16), "rep").astype(jnp.float32),
        lax.psum(part_up_bias.astype(jnp.bfloat16), "rep").astype(jnp.float32),
        lax.psum(part_down.astype(jnp.bfloat16), "rep").astype(jnp.float32),
        lax.psum(part_down_bias.astype(jnp.bfloat16), "rep").astype(jnp.float32),
    )
    return (
        output.astype(bf16),
        grad_inputs,
        part_gain_one,
        part_shift_one,
        part_packed,
        part_pair,
        part_proj,
        part_proj_bias,
        part_gain_two,
        part_shift_two,
        part_up,
        part_up_bias,
        part_down,
        part_down_bias,
    )


AXES = ("rep", "shard")


class Grid:
    def __init__(self):
        rep = lax.axis_index("rep")
        self.y = lax.axis_index("shard")
        self.core = rep % 2
        self.x = (rep // 2) % 2
        self.z_low = (rep // 4) % 2
        self.z_high = rep // 8

    def swap(self, array, bit):
        return lax.ppermute(array, AXES, [(i, i ^ bit) for i in range(32)])


Y_BIT, CORE_BIT, X_BIT, LOW_BIT, HIGH_BIT = 1, 2, 4, 8, 16


def half_of(array, index):
    return lax.dynamic_index_in_dim(array, index, 0, keepdims=False)


def join(own, other, index):
    first = index == 0
    return jnp.stack([jnp.where(first, own, other), jnp.where(first, other, own)])


def transpose_pairs(grid, array):
    pairs = []
    for i in range(0, 32, 4):
        pairs += [(i + 1, i + 2), (i + 2, i + 1)]
    moved = lax.ppermute(array, AXES, pairs)
    return jnp.where(grid.y == grid.core, array, moved)


def whole_weight(grid, own):
    rows, columns = own.shape
    quarter = rows // 4
    place = grid.core * 2 + grid.x
    sent = lax.dynamic_slice_in_dim(own, place * quarter, quarter, 0)
    first = grid.swap(sent, Y_BIT)
    second = grid.swap(first, X_BIT)
    half = join(first, second, grid.x).reshape(2 * quarter, columns)
    other = grid.swap(half, CORE_BIT)
    base = (1 - grid.y) * rows
    full = jnp.zeros((2 * rows, columns), own.dtype)
    full = lax.dynamic_update_slice_in_dim(full, own, grid.y * rows, 0)
    full = lax.dynamic_update_slice_in_dim(full, half, base + grid.core * 2 * quarter, 0)
    return lax.dynamic_update_slice_in_dim(
        full, other, base + (1 - grid.core) * 2 * quarter, 0
    )


def reduced_gradient(grid, features, grads):
    f32, bf16 = jnp.float32, jnp.bfloat16
    tok_rows, width = features.shape
    columns = grads.shape[1]
    split = features.reshape(tok_rows, 2, 2, width // 4)

    def part(side, core):
        chosen = lax.dynamic_index_in_dim(split, side, 1, keepdims=False)
        chosen = lax.dynamic_index_in_dim(chosen, core, 1, keepdims=False)
        return jnp.einsum("td,te->de", chosen, grads, preferred_element_type=f32)

    far_side, far_core = 1 - grid.y, 1 - grid.core
    got_far = grid.swap(part(far_side, far_core).astype(bf16), CORE_BIT)
    got_near = grid.swap(part(grid.y, far_core).astype(bf16), CORE_BIT)
    far = (part(far_side, grid.core) + got_far.astype(f32)).astype(bf16)
    got = grid.swap(far, Y_BIT)
    total = (part(grid.y, grid.core) + got_near.astype(f32) + got.astype(f32)).astype(bf16)
    total = total.reshape(2, 2, 2, width // 32, columns)
    for index, bit in ((grid.x, X_BIT), (grid.z_low, LOW_BIT), (grid.z_high, HIGH_BIT)):
        got = grid.swap(half_of(total, 1 - index), bit)
        total = (half_of(total, index).astype(f32) + got.astype(f32)).astype(bf16)
    for index, bit in (
        (grid.z_high, HIGH_BIT),
        (grid.z_low, LOW_BIT),
        (grid.x, X_BIT),
        (grid.core, CORE_BIT),
    ):
        total = join(total, grid.swap(total, bit), index)
    return total.reshape(width // 2, columns).astype(f32)


def summed_everywhere(grid, vector):
    for bit in (CORE_BIT, Y_BIT, X_BIT, LOW_BIT, HIGH_BIT):
        vector = vector + grid.swap(vector, bit)
    return vector


def pair_scores(query_heads, key_heads, first_row, key_pos):
    tok_rows, heads_count, head_size = query_heads.shape
    scores = jnp.einsum(
        "qhd,khd->hqk", query_heads, key_heads, preferred_element_type=jnp.float32
    ) * head_size ** (-0.5)
    slopes = 2.0 ** (-8.0 * (jnp.arange(heads_count, dtype=jnp.float32) + 1.0) / heads_count)
    query_pos = first_row + jnp.arange(tok_rows, dtype=jnp.int32)
    distance = (query_pos[:, None] - key_pos[None, :]).astype(jnp.float32)
    scores = scores - slopes[:, None, None] * distance[None]
    causal = (key_pos[None, :] <= query_pos[:, None])[None]
    return jnp.where(causal, scores, -1e30)


def attention_forward(query_b, keys_b, values_b, first_row, key_pos):
    f32, bf16 = jnp.float32, jnp.bfloat16
    tok_rows, width = query_b.shape
    query_heads = query_b.reshape(tok_rows, HEADS, HEAD)
    key_heads = keys_b.reshape(-1, HEADS, HEAD)
    value_heads = values_b.reshape(-1, HEADS, HEAD)
    scores = pair_scores(query_heads, key_heads, first_row, key_pos)
    row_max = jnp.max(scores, axis=-1, keepdims=True)
    exp_terms = jnp.exp(scores - row_max)
    row_total = jnp.sum(exp_terms, axis=-1, keepdims=True)
    logsum = row_max + jnp.log(row_total)
    probs_b = (exp_terms / row_total).astype(bf16)
    mixed = jnp.einsum("hqk,khd->qhd", probs_b, value_heads, preferred_element_type=f32)
    return mixed.reshape(tok_rows, width).astype(bf16), logsum


def attention_backward(query_b, keys_b, values_b, grad_mixed_b, logsum, first_row, key_pos):
    f32, bf16 = jnp.float32, jnp.bfloat16
    tok_rows, width = query_b.shape
    query_heads = query_b.reshape(tok_rows, HEADS, HEAD)
    key_heads = keys_b.reshape(-1, HEADS, HEAD)
    value_heads = values_b.reshape(-1, HEADS, HEAD)
    grad_mixed_heads = grad_mixed_b.reshape(tok_rows, HEADS, HEAD)
    scores = pair_scores(query_heads, key_heads, first_row, key_pos)
    attn_probs = jnp.exp(scores - logsum)
    probs_b = attn_probs.astype(bf16)
    grad_probs = jnp.einsum(
        "qhd,khd->hqk", grad_mixed_heads, value_heads, preferred_element_type=f32
    )
    row_delta = jnp.sum(attn_probs * grad_probs, axis=-1, keepdims=True)
    grad_scores_b = (attn_probs * (grad_probs - row_delta)).astype(bf16)
    scale = HEAD ** (-0.5)
    grad_query = (
        jnp.einsum("hqk,khd->qhd", grad_scores_b, key_heads, preferred_element_type=f32) * scale
    ).reshape(tok_rows, width)
    key_terms = (
        jnp.einsum("hqk,qhd->khd", grad_scores_b, query_heads, preferred_element_type=f32) * scale
    ).reshape(-1, width)
    value_terms = jnp.einsum(
        "hqk,qhd->khd", probs_b, grad_mixed_heads, preferred_element_type=f32
    ).reshape(-1, width)
    return grad_query.astype(bf16), key_terms.astype(bf16), value_terms.astype(bf16)


def paired_device(
    tokens,
    ln1_gain,
    ln1_bias,
    qkv_weight,
    qv_bias,
    proj_weight,
    proj_bias,
    ln2_gain,
    ln2_bias,
    fc1_weight,
    fc1_bias,
    fc2_weight,
    fc2_bias,
    cotangent,
):
    f32 = jnp.float32
    bf16 = jnp.bfloat16
    grid = Grid()
    tok_rows, width = tokens.shape
    vectors = (ln1_gain, ln1_bias, qv_bias, proj_bias, ln2_gain, ln2_bias, fc1_bias, fc2_bias)
    own_vectors = jnp.concatenate(vectors).reshape(-1, 128)
    both = join(own_vectors, grid.swap(own_vectors, Y_BIT), grid.y).reshape(2, -1).astype(f32)
    full_vectors, start = [], 0
    for vector in vectors:
        full_vectors.append(both[:, start : start + vector.shape[0]].reshape(-1))
        start += vector.shape[0]
    gain_one, shift_one, pair_bias, out_bias, gain_two, shift_two, up_bias, down_bias = full_vectors
    tokens = transpose_pairs(grid, tokens)
    packed_w = whole_weight(grid, qkv_weight)
    proj_w = whole_weight(grid, proj_weight)
    up_w = whole_weight(grid, fc1_weight)
    down_w = whole_weight(grid, fc2_weight)
    cotangent = transpose_pairs(grid, cotangent)

    first_row = grid.core * tok_rows
    row_ids = jnp.arange(tok_rows, dtype=jnp.int32)
    key_pos = jnp.concatenate([first_row + row_ids, (1 - grid.core) * tok_rows + row_ids])
    inputs = tokens.astype(f32)
    normed_one, scaled_one, inverse_one = normalize(inputs, gain_one, shift_one)
    normed_one_b = normed_one.astype(bf16)
    packed = jnp.dot(normed_one_b, packed_w, preferred_element_type=f32)
    query_b = (packed[:, :width] + pair_bias[:width]).astype(bf16)
    keys_b = packed[:, width : 2 * width].astype(bf16)
    values_b = (packed[:, 2 * width :] + pair_bias[width:]).astype(bf16)
    keys_b = jnp.concatenate([keys_b, grid.swap(keys_b, CORE_BIT)])
    values_b = jnp.concatenate([values_b, grid.swap(values_b, CORE_BIT)])
    mixed_b, logsum = attention_forward(query_b, keys_b, values_b, first_row, key_pos)
    resid = inputs + jnp.dot(mixed_b, proj_w, preferred_element_type=f32) + out_bias
    normed_two, scaled_two, inverse_two = normalize(resid, gain_two, shift_two)
    normed_two_b = normed_two.astype(bf16)
    hidden = jnp.dot(normed_two_b, up_w, preferred_element_type=f32) + up_bias
    active_b = tanh_gelu(hidden).astype(bf16)
    cotan = cotangent.astype(f32)
    grad_down = reduced_gradient(grid, active_b, cotangent)
    grad_active = jnp.einsum("td,fd->tf", cotangent, down_w, preferred_element_type=f32)
    unused_value, gelu_back = jax.vjp(tanh_gelu, hidden)
    grad_hidden = gelu_back(grad_active)[0]
    grad_hidden_b = grad_hidden.astype(bf16)
    grad_up = reduced_gradient(grid, normed_two_b, grad_hidden_b)
    output = resid + jnp.dot(active_b, down_w, preferred_element_type=f32) + down_bias
    output = transpose_pairs(grid, output.astype(bf16))
    grad_norm_two = jnp.einsum("tf,df->td", grad_hidden_b, up_w, preferred_element_type=f32)
    grad_resid = cotan + normal_back(grad_norm_two, scaled_two, inverse_two, gain_two)
    grad_branch_b = grad_resid.astype(bf16)
    grad_proj = reduced_gradient(grid, mixed_b, grad_branch_b)
    grad_mixed_b = jnp.einsum(
        "te,de->td", grad_branch_b, proj_w, preferred_element_type=f32
    ).astype(bf16)
    grad_query_b, key_terms, value_terms = attention_backward(
        query_b, keys_b, values_b, grad_mixed_b, logsum, first_row, key_pos
    )
    grad_keys_b = (
        key_terms[:tok_rows].astype(f32) + grid.swap(key_terms[tok_rows:], CORE_BIT).astype(f32)
    ).astype(bf16)
    grad_values_b = (
        value_terms[:tok_rows].astype(f32)
        + grid.swap(value_terms[tok_rows:], CORE_BIT).astype(f32)
    ).astype(bf16)
    grad_packed_b = jnp.concatenate([grad_query_b, grad_keys_b, grad_values_b], axis=1)
    grad_packed = reduced_gradient(grid, normed_one_b, grad_packed_b)
    grad_norm_one = jnp.einsum("te,de->td", grad_packed_b, packed_w, preferred_element_type=f32)
    grad_inputs = grad_resid + normal_back(grad_norm_one, scaled_one, inverse_one, gain_one)
    grad_inputs = jnp.where(
        grid.y == grid.core,
        grad_inputs,
        transpose_pairs(grid, grad_inputs.astype(bf16)).astype(f32),
    )
    sums = (
        jnp.sum(grad_norm_one * scaled_one, axis=0),
        jnp.sum(grad_norm_one, axis=0),
        jnp.sum(grad_query_b.astype(f32), axis=0),
        jnp.sum(grad_values_b.astype(f32), axis=0),
        jnp.sum(grad_branch_b.astype(f32), axis=0),
        jnp.sum(grad_norm_two * scaled_two, axis=0),
        jnp.sum(grad_norm_two, axis=0),
        jnp.sum(grad_hidden_b.astype(f32), axis=0),
        jnp.sum(cotan, axis=0),
    )
    lengths = (width, width, 2 * width, width, width, width, sums[7].shape[0], width)
    totals = summed_everywhere(grid, jnp.concatenate(sums).reshape(-1, 128)).reshape(-1)
    owned, start = [], 0
    for length in lengths:
        owned.append(owned_part(totals[start : start + length], 2))
        start += length
    return (
        output,
        grad_inputs,
        owned[0],
        owned[1],
        grad_packed,
        owned[2],
        grad_proj,
        owned[3],
        owned[4],
        owned[5],
        grad_up,
        owned[6],
        grad_down,
        owned[7],
    )


def solution(mesh):
    two_way = mesh.shape["shard"] == 2 and mesh.shape["rep"] == 16
    return jax.shard_map(
        paired_device if two_way else per_device,
        mesh=mesh,
        in_specs=(
            P(("rep", "shard"), None),
            P("shard"),
            P("shard"),
            P("shard", None),
            P("shard"),
            P("shard", None),
            P("shard"),
            P("shard"),
            P("shard"),
            P("shard", None),
            P("shard"),
            P("shard", None),
            P("shard"),
            P(("rep", "shard"), None),
        ),
        out_specs=(
            P(("rep", "shard"), None),
            P(("rep", "shard"), None),
            P("shard"),
            P("shard"),
            P("shard", None),
            P("shard"),
            P("shard", None),
            P("shard"),
            P("shard"),
            P("shard"),
            P("shard", None),
            P("shard"),
            P("shard", None),
            P("shard"),
        ),
        check_vma=False,
    )
```

```python
import jax
import jax.numpy as jnp
from jax import lax
from jax.sharding import PartitionSpec as P

HEADS = 16
HEAD = 64


def normalize(values_in, gain_vec, shift_vec):
    centered = values_in - jnp.mean(values_in, axis=-1, keepdims=True)
    inverse = lax.rsqrt(jnp.mean(centered * centered, axis=-1, keepdims=True) + 1e-05)
    scaled = centered * inverse
    return (scaled * gain_vec + shift_vec, scaled, inverse)


def normal_back(grad_in, scaled, inverse, gain_vec):
    inner = grad_in * gain_vec
    return inverse * (
        inner
        - jnp.mean(inner, axis=-1, keepdims=True)
        - scaled * jnp.mean(inner * scaled, axis=-1, keepdims=True)
    )


def tanh_gelu(values_in):
    return jax.nn.gelu(values_in, approximate=True)


def owned_part(vector, pieces):
    length = vector.shape[0] // pieces
    return lax.dynamic_slice_in_dim(vector, lax.axis_index("shard") * length, length, 0)


def group_vectors(gain_sum, shift_sum):
    pieces = lax.axis_size("shard")
    summed_gain, summed_shift = lax.psum((gain_sum, shift_sum), "shard")
    return (owned_part(summed_gain, pieces), owned_part(summed_shift, pieces))


def score_block(query_heads, key_heads, first_row):
    tok_rows, heads_count, head_size = query_heads.shape
    seq_len = key_heads.shape[0]
    scores = jnp.einsum(
        "qhd,khd->hqk", query_heads, key_heads, preferred_element_type=jnp.float32
    ) * head_size ** (-0.5)
    slopes = 2.0 ** (-8.0 * (jnp.arange(heads_count, dtype=jnp.float32) + 1.0) / heads_count)
    query_pos = first_row + jnp.arange(tok_rows, dtype=jnp.int32)
    key_pos = jnp.arange(seq_len, dtype=jnp.int32)
    distance = (query_pos[:, None] - key_pos[None, :]).astype(jnp.float32)
    scores = scores - slopes[:, None, None] * distance[None]
    causal = (key_pos[None, :] <= query_pos[:, None])[None]
    return jnp.where(causal, scores, -1e30)


def per_device(
    tokens,
    ln1_gain,
    ln1_bias,
    qkv_weight,
    qv_bias,
    proj_weight,
    proj_bias,
    ln2_gain,
    ln2_bias,
    fc1_weight,
    fc1_bias,
    fc2_weight,
    fc2_bias,
    cotangent,
):
    f32 = jnp.float32
    bf16 = jnp.bfloat16
    tok_rows, width = tokens.shape
    pieces = lax.axis_size("shard")
    first_row = lax.axis_index("shard") * tok_rows
    gathered = (
        lax.all_gather(ln1_gain, "shard", axis=0, tiled=True),
        lax.all_gather(ln1_bias, "shard", axis=0, tiled=True),
        lax.all_gather(qkv_weight, "shard", axis=0, tiled=True),
        lax.all_gather(qv_bias, "shard", axis=0, tiled=True),
        lax.all_gather(proj_weight, "shard", axis=0, tiled=True),
        lax.all_gather(proj_bias, "shard", axis=0, tiled=True),
        lax.all_gather(ln2_gain, "shard", axis=0, tiled=True),
        lax.all_gather(ln2_bias, "shard", axis=0, tiled=True),
        lax.all_gather(fc1_weight, "shard", axis=0, tiled=True),
        lax.all_gather(fc1_bias, "shard", axis=0, tiled=True),
        lax.all_gather(fc2_weight, "shard", axis=0, tiled=True),
        lax.all_gather(fc2_bias, "shard", axis=0, tiled=True),
    )
    inputs = tokens.astype(f32)
    normed_one, scaled_one, inverse_one = normalize(
        inputs, gathered[0].astype(f32), gathered[1].astype(f32)
    )
    normed_one_b = normed_one.astype(bf16)
    packed = jnp.dot(normed_one_b, gathered[2], preferred_element_type=f32)
    pair_bias = gathered[3].astype(f32)
    query_b = (packed[:, :width] + pair_bias[:width]).astype(bf16)
    keys_b = packed[:, width : 2 * width].astype(bf16)
    values_b = (packed[:, 2 * width :] + pair_bias[width:]).astype(bf16)
    all_keys, all_values = (
        lax.all_gather(keys_b, "shard", axis=0, tiled=True),
        lax.all_gather(values_b, "shard", axis=0, tiled=True),
    )
    query_heads = query_b.reshape(tok_rows, HEADS, HEAD)
    key_heads = all_keys.reshape(-1, HEADS, HEAD)
    value_heads = all_values.reshape(-1, HEADS, HEAD)
    scores = score_block(query_heads, key_heads, first_row)
    row_max = jnp.max(scores, axis=-1, keepdims=True)
    exp_terms = jnp.exp(scores - row_max)
    row_total = jnp.sum(exp_terms, axis=-1, keepdims=True)
    logsum = row_max + jnp.log(row_total)
    probs_b = (exp_terms / row_total).astype(bf16)
    mixed_b = (
        jnp.einsum("hqk,khd->qhd", probs_b, value_heads, preferred_element_type=f32)
        .reshape(tok_rows, width)
        .astype(bf16)
    )
    resid = (
        inputs + jnp.dot(mixed_b, gathered[4], preferred_element_type=f32) + gathered[5].astype(f32)
    )
    normed_two, scaled_two, inverse_two = normalize(
        resid, gathered[6].astype(f32), gathered[7].astype(f32)
    )
    normed_two_b = normed_two.astype(bf16)
    hidden = jnp.dot(normed_two_b, gathered[8], preferred_element_type=f32) + gathered[9].astype(
        f32
    )
    active_b = tanh_gelu(hidden).astype(bf16)
    output = (
        resid
        + jnp.dot(active_b, gathered[10], preferred_element_type=f32)
        + gathered[11].astype(f32)
    )
    cotan = cotangent.astype(f32)
    grad_active = jnp.einsum("td,fd->tf", cotangent, gathered[10], preferred_element_type=f32)
    unused_value, gelu_back = jax.vjp(tanh_gelu, hidden)
    grad_hidden_b = gelu_back(grad_active)[0].astype(bf16)
    grad_norm_two = jnp.einsum("tf,df->td", grad_hidden_b, gathered[8], preferred_element_type=f32)
    grad_gain_two = jnp.sum(grad_norm_two * scaled_two, axis=0)
    grad_shift_two = jnp.sum(grad_norm_two, axis=0)
    grad_resid = cotan + normal_back(
        grad_norm_two, scaled_two, inverse_two, gathered[6].astype(f32)
    )
    owned_two, owned_active = (
        lax.all_to_all(normed_two_b, "shard", split_axis=1, concat_axis=0, tiled=True),
        lax.all_to_all(active_b, "shard", split_axis=1, concat_axis=0, tiled=True),
    )
    group_cotan, group_hidden = (
        lax.all_gather(cotangent, "shard", axis=0, tiled=True),
        lax.all_gather(grad_hidden_b, "shard", axis=0, tiled=True),
    )
    part_down = jnp.einsum("tf,td->fd", owned_active, group_cotan, preferred_element_type=f32)
    part_up = jnp.einsum("td,tf->df", owned_two, group_hidden, preferred_element_type=f32)
    part_down_bias = owned_part(jnp.sum(group_cotan.astype(f32), axis=0), pieces)
    part_up_bias = owned_part(jnp.sum(group_hidden.astype(f32), axis=0), pieces)
    part_gain_two, part_shift_two = group_vectors(grad_gain_two, grad_shift_two)
    grad_branch_b = grad_resid.astype(bf16)
    grad_mixed_b = jnp.einsum(
        "te,de->td", grad_branch_b, gathered[4], preferred_element_type=f32
    ).astype(bf16)
    grad_mixed_heads = grad_mixed_b.reshape(tok_rows, HEADS, HEAD)
    scores = score_block(query_heads, key_heads, first_row)
    attn_probs = jnp.exp(scores - logsum)
    probs_b = attn_probs.astype(bf16)
    grad_probs = jnp.einsum(
        "qhd,khd->hqk", grad_mixed_heads, value_heads, preferred_element_type=f32
    )
    row_delta = jnp.sum(attn_probs * grad_probs, axis=-1, keepdims=True)
    grad_scores_b = (attn_probs * (grad_probs - row_delta)).astype(bf16)
    score_scale = HEAD ** (-0.5)
    grad_query_b = (
        (
            jnp.einsum("hqk,khd->qhd", grad_scores_b, key_heads, preferred_element_type=f32)
            * score_scale
        )
        .reshape(tok_rows, width)
        .astype(bf16)
    )
    key_terms = (
        jnp.einsum("hqk,qhd->khd", grad_scores_b, query_heads, preferred_element_type=f32)
        * score_scale
    ).reshape(-1, width)
    value_terms = jnp.einsum(
        "hqk,qhd->khd", probs_b, grad_mixed_heads, preferred_element_type=f32
    ).reshape(-1, width)
    grad_keys, grad_values = (
        lax.psum_scatter(
            key_terms.astype(jnp.bfloat16), "shard", scatter_dimension=0, tiled=True
        ).astype(jnp.float32),
        lax.psum_scatter(
            value_terms.astype(jnp.bfloat16), "shard", scatter_dimension=0, tiled=True
        ).astype(jnp.float32),
    )
    grad_values_b = grad_values.astype(bf16)
    grad_packed_b = jnp.concatenate([grad_query_b, grad_keys.astype(bf16), grad_values_b], axis=1)
    grad_norm_one = jnp.einsum("te,de->td", grad_packed_b, gathered[2], preferred_element_type=f32)
    grad_gain_one = jnp.sum(grad_norm_one * scaled_one, axis=0)
    grad_shift_one = jnp.sum(grad_norm_one, axis=0)
    grad_inputs = grad_resid + normal_back(
        grad_norm_one, scaled_one, inverse_one, gathered[0].astype(f32)
    )
    owned_one, owned_mixed = (
        lax.all_to_all(normed_one_b, "shard", split_axis=1, concat_axis=0, tiled=True),
        lax.all_to_all(mixed_b, "shard", split_axis=1, concat_axis=0, tiled=True),
    )
    group_packed, group_branch = (
        lax.all_gather(grad_packed_b, "shard", axis=0, tiled=True),
        lax.all_gather(grad_branch_b, "shard", axis=0, tiled=True),
    )
    part_packed = jnp.einsum("td,te->de", owned_one, group_packed, preferred_element_type=f32)
    part_proj = jnp.einsum("td,te->de", owned_mixed, group_branch, preferred_element_type=f32)
    packed_sums = jnp.sum(group_packed.astype(f32), axis=0)
    part_pair = owned_part(jnp.concatenate([packed_sums[:width], packed_sums[2 * width :]]), pieces)
    part_proj_bias = owned_part(jnp.sum(group_branch.astype(f32), axis=0), pieces)
    part_gain_one, part_shift_one = group_vectors(grad_gain_one, grad_shift_one)
    (
        part_gain_one,
        part_shift_one,
        part_packed,
        part_pair,
        part_proj,
        part_proj_bias,
        part_gain_two,
        part_shift_two,
        part_up,
        part_up_bias,
        part_down,
        part_down_bias,
    ) = (
        lax.psum(part_gain_one.astype(jnp.bfloat16), "rep").astype(jnp.float32),
        lax.psum(part_shift_one.astype(jnp.bfloat16), "rep").astype(jnp.float32),
        lax.psum(part_packed.astype(jnp.bfloat16), "rep").astype(jnp.float32),
        lax.psum(part_pair.astype(jnp.bfloat16), "rep").astype(jnp.float32),
        lax.psum(part_proj.astype(jnp.bfloat16), "rep").astype(jnp.float32),
        lax.psum(part_proj_bias.astype(jnp.bfloat16), "rep").astype(jnp.float32),
        lax.psum(part_gain_two.astype(jnp.bfloat16), "rep").astype(jnp.float32),
        lax.psum(part_shift_two.astype(jnp.bfloat16), "rep").astype(jnp.float32),
        lax.psum(part_up.astype(jnp.bfloat16), "rep").astype(jnp.float32),
        lax.psum(part_up_bias.astype(jnp.bfloat16), "rep").astype(jnp.float32),
        lax.psum(part_down.astype(jnp.bfloat16), "rep").astype(jnp.float32),
        lax.psum(part_down_bias.astype(jnp.bfloat16), "rep").astype(jnp.float32),
    )
    return (
        output.astype(bf16),
        grad_inputs,
        part_gain_one,
        part_shift_one,
        part_packed,
        part_pair,
        part_proj,
        part_proj_bias,
        part_gain_two,
        part_shift_two,
        part_up,
        part_up_bias,
        part_down,
        part_down_bias,
    )


AXES = ("rep", "shard")


class Grid:
    def __init__(self):
        rep = lax.axis_index("rep")
        self.y = lax.axis_index("shard")
        self.core = rep % 2
        self.x = (rep // 2) % 2
        self.z_low = (rep // 4) % 2
        self.z_high = rep // 8
        self.bits = {
            "core": (self.core, CORE_BIT),
            "x": (self.x, X_BIT),
            "low": (self.z_low, LOW_BIT),
            "high": (self.z_high, HIGH_BIT),
        }

    def swap(self, array, bit):
        return lax.ppermute(array, AXES, [(i, i ^ bit) for i in range(32)])


Y_BIT, CORE_BIT, X_BIT, LOW_BIT, HIGH_BIT = 1, 2, 4, 8, 16


def half_of(array, index):
    return lax.dynamic_index_in_dim(array, index, 0, keepdims=False)


def join(own, other, index):
    first = index == 0
    return jnp.stack([jnp.where(first, own, other), jnp.where(first, other, own)])


def transpose_pairs(grid, array):
    pairs = []
    for i in range(0, 32, 4):
        pairs += [(i + 1, i + 2), (i + 2, i + 1)]
    moved = lax.ppermute(array, AXES, pairs)
    return jnp.where(grid.y == grid.core, array, moved)


def quarter_of(grid, own):
    quarter = own.shape[0] // 4
    place = grid.core * 2 + grid.x
    return lax.dynamic_slice_in_dim(own, place * quarter, quarter, 0)


def whole_weight(grid, own, first):
    rows, columns = own.shape
    quarter = rows // 4
    second = grid.swap(first, X_BIT)
    half = join(first, second, grid.x).reshape(2 * quarter, columns)
    other = grid.swap(half, CORE_BIT)
    base = (1 - grid.y) * rows
    full = jnp.zeros((2 * rows, columns), own.dtype)
    full = lax.dynamic_update_slice_in_dim(full, own, grid.y * rows, 0)
    full = lax.dynamic_update_slice_in_dim(full, half, base + grid.core * 2 * quarter, 0)
    return lax.dynamic_update_slice_in_dim(
        full, other, base + (1 - grid.core) * 2 * quarter, 0
    )


def begin_sum(grid, features, grads):
    f32, bf16 = jnp.float32, jnp.bfloat16
    tok_rows, width = features.shape
    split = features.reshape(tok_rows, 2, 2, width // 4)

    def part(side, core):
        chosen = lax.dynamic_index_in_dim(split, side, 1, keepdims=False)
        chosen = lax.dynamic_index_in_dim(chosen, core, 1, keepdims=False)
        return jnp.einsum("td,te->de", chosen, grads, preferred_element_type=f32)

    far_side, far_core = 1 - grid.y, 1 - grid.core
    got_far = grid.swap(part(far_side, far_core).astype(bf16), CORE_BIT)
    got_near = grid.swap(part(grid.y, far_core).astype(bf16), CORE_BIT)
    far = (part(far_side, grid.core) + got_far.astype(f32)).astype(bf16)
    return far, (part(grid.y, grid.core) + got_near.astype(f32)).astype(bf16)


def add_group(near, got):
    rows, columns = near.shape
    total = (near.astype(jnp.float32) + got.astype(jnp.float32)).astype(jnp.bfloat16)
    return total.reshape(2, 2, 2, rows // 8, columns)


def scatter(grid, total, names):
    for name in names:
        index, bit = grid.bits[name]
        got = grid.swap(half_of(total, 1 - index), bit)
        total = (half_of(total, index).astype(jnp.float32) + got.astype(jnp.float32)).astype(
            jnp.bfloat16
        )
    return total


def gather(grid, total, names):
    for name in names:
        index, bit = grid.bits[name]
        total = join(total, grid.swap(total, bit), index)
    return total


def as_rows(total):
    return total.reshape(-1, total.shape[-1]).astype(jnp.float32)


def summed_everywhere(grid, vector):
    for bit in (CORE_BIT, Y_BIT, X_BIT, LOW_BIT, HIGH_BIT):
        vector = vector + grid.swap(vector, bit)
    return vector


def pair_scores(query_heads, key_heads, first_row, key_pos):
    tok_rows, heads_count, head_size = query_heads.shape
    scores = jnp.einsum(
        "qhd,khd->hqk", query_heads, key_heads, preferred_element_type=jnp.float32
    ) * head_size ** (-0.5)
    slopes = 2.0 ** (-8.0 * (jnp.arange(heads_count, dtype=jnp.float32) + 1.0) / heads_count)
    query_pos = first_row + jnp.arange(tok_rows, dtype=jnp.int32)
    distance = (query_pos[:, None] - key_pos[None, :]).astype(jnp.float32)
    scores = scores - slopes[:, None, None] * distance[None]
    causal = (key_pos[None, :] <= query_pos[:, None])[None]
    return jnp.where(causal, scores, -1e30)


def attention_forward(query_b, keys_b, values_b, first_row, key_pos):
    f32, bf16 = jnp.float32, jnp.bfloat16
    tok_rows, width = query_b.shape
    query_heads = query_b.reshape(tok_rows, HEADS, HEAD)
    key_heads = keys_b.reshape(-1, HEADS, HEAD)
    value_heads = values_b.reshape(-1, HEADS, HEAD)
    scores = pair_scores(query_heads, key_heads, first_row, key_pos)
    row_max = jnp.max(scores, axis=-1, keepdims=True)
    exp_terms = jnp.exp(scores - row_max)
    row_total = jnp.sum(exp_terms, axis=-1, keepdims=True)
    logsum = row_max + jnp.log(row_total)
    probs_b = (exp_terms / row_total).astype(bf16)
    mixed = jnp.einsum("hqk,khd->qhd", probs_b, value_heads, preferred_element_type=f32)
    return mixed.reshape(tok_rows, width).astype(bf16), logsum


def attention_scores_backward(query_b, keys_b, values_b, grad_mixed_b, logsum, first_row, key_pos):
    f32, bf16 = jnp.float32, jnp.bfloat16
    tok_rows, width = query_b.shape
    query_heads = query_b.reshape(tok_rows, HEADS, HEAD)
    key_heads = keys_b.reshape(-1, HEADS, HEAD)
    value_heads = values_b.reshape(-1, HEADS, HEAD)
    grad_mixed_heads = grad_mixed_b.reshape(tok_rows, HEADS, HEAD)
    scores = pair_scores(query_heads, key_heads, first_row, key_pos)
    attn_probs = jnp.exp(scores - logsum)
    probs_b = attn_probs.astype(bf16)
    grad_probs = jnp.einsum(
        "qhd,khd->hqk", grad_mixed_heads, value_heads, preferred_element_type=f32
    )
    row_delta = jnp.sum(attn_probs * grad_probs, axis=-1, keepdims=True)
    grad_scores_b = (attn_probs * (grad_probs - row_delta)).astype(bf16)
    return probs_b, grad_scores_b


def attention_products_backward(query_b, keys_b, grad_mixed_b, probs_b, grad_scores_b):
    f32, bf16 = jnp.float32, jnp.bfloat16
    tok_rows, width = query_b.shape
    query_heads = query_b.reshape(tok_rows, HEADS, HEAD)
    key_heads = keys_b.reshape(-1, HEADS, HEAD)
    grad_mixed_heads = grad_mixed_b.reshape(tok_rows, HEADS, HEAD)
    scale = HEAD ** (-0.5)
    grad_query = (
        jnp.einsum("hqk,khd->qhd", grad_scores_b, key_heads, preferred_element_type=f32) * scale
    ).reshape(tok_rows, width)
    key_terms = (
        jnp.einsum("hqk,qhd->khd", grad_scores_b, query_heads, preferred_element_type=f32) * scale
    ).reshape(-1, width)
    value_terms = jnp.einsum(
        "hqk,qhd->khd", probs_b, grad_mixed_heads, preferred_element_type=f32
    ).reshape(-1, width)
    return grad_query.astype(bf16), key_terms.astype(bf16), value_terms.astype(bf16)


def paired_device(
    tokens,
    ln1_gain,
    ln1_bias,
    qkv_weight,
    qv_bias,
    proj_weight,
    proj_bias,
    ln2_gain,
    ln2_bias,
    fc1_weight,
    fc1_bias,
    fc2_weight,
    fc2_bias,
    cotangent,
):
    f32 = jnp.float32
    bf16 = jnp.bfloat16
    grid = Grid()
    tok_rows, width = tokens.shape
    vectors = (ln1_gain, ln1_bias, qv_bias, proj_bias, ln2_gain, ln2_bias, fc1_bias, fc2_bias)
    own_vectors = jnp.concatenate(vectors).reshape(-1, 128)
    both = join(own_vectors, grid.swap(own_vectors, Y_BIT), grid.y).reshape(2, -1).astype(f32)
    full_vectors, start = [], 0
    for vector in vectors:
        full_vectors.append(both[:, start : start + vector.shape[0]].reshape(-1))
        start += vector.shape[0]
    gain_one, shift_one, pair_bias, out_bias, gain_two, shift_two, up_bias, down_bias = full_vectors
    tokens = transpose_pairs(grid, tokens)
    packed_first = grid.swap(quarter_of(grid, qkv_weight), Y_BIT)
    sent_proj, sent_up, sent_down = (
        quarter_of(grid, weight) for weight in (proj_weight, fc1_weight, fc2_weight)
    )
    packed_first, sent_proj, sent_up = lax.optimization_barrier(
        (packed_first, sent_proj, sent_up)
    )
    proj_first = grid.swap(sent_proj, Y_BIT)
    up_first = grid.swap(sent_up, Y_BIT)
    up_first, sent_down = lax.optimization_barrier((up_first, sent_down))
    down_first = grid.swap(sent_down, Y_BIT)
    down_first, cotangent = lax.optimization_barrier((down_first, cotangent))
    packed_w = whole_weight(grid, qkv_weight, packed_first)
    proj_w = whole_weight(grid, proj_weight, proj_first)
    up_w = whole_weight(grid, fc1_weight, up_first)
    down_w = whole_weight(grid, fc2_weight, down_first)
    cotangent = transpose_pairs(grid, cotangent)

    first_row = grid.core * tok_rows
    row_ids = jnp.arange(tok_rows, dtype=jnp.int32)
    key_pos = jnp.concatenate([first_row + row_ids, (1 - grid.core) * tok_rows + row_ids])
    inputs = tokens.astype(f32)
    normed_one, scaled_one, inverse_one = normalize(inputs, gain_one, shift_one)
    normed_one_b = normed_one.astype(bf16)
    packed = jnp.dot(normed_one_b, packed_w, preferred_element_type=f32)
    query_b = (packed[:, :width] + pair_bias[:width]).astype(bf16)
    keys_b = packed[:, width : 2 * width].astype(bf16)
    values_b = (packed[:, 2 * width :] + pair_bias[width:]).astype(bf16)
    keys_b = jnp.concatenate([keys_b, grid.swap(keys_b, CORE_BIT)])
    values_b = jnp.concatenate([values_b, grid.swap(values_b, CORE_BIT)])
    mixed_b, logsum = attention_forward(query_b, keys_b, values_b, first_row, key_pos)
    resid = inputs + jnp.dot(mixed_b, proj_w, preferred_element_type=f32) + out_bias
    normed_two, scaled_two, inverse_two = normalize(resid, gain_two, shift_two)
    normed_two_b = normed_two.astype(bf16)
    hidden = jnp.dot(normed_two_b, up_w, preferred_element_type=f32) + up_bias
    active_b = tanh_gelu(hidden).astype(bf16)
    cotan = cotangent.astype(f32)
    down_far, down_near = begin_sum(grid, active_b, cotangent)
    down_far, cotangent, hidden = lax.optimization_barrier((down_far, cotangent, hidden))
    down_got = grid.swap(down_far, Y_BIT)
    grad_active = jnp.einsum("td,fd->tf", cotangent, down_w, preferred_element_type=f32)
    unused_value, gelu_back = jax.vjp(tanh_gelu, hidden)
    grad_hidden = gelu_back(grad_active)[0]
    grad_hidden_b = grad_hidden.astype(bf16)
    up_far, up_near = begin_sum(grid, normed_two_b, grad_hidden_b)
    output = resid + jnp.dot(active_b, down_w, preferred_element_type=f32) + down_bias
    output = transpose_pairs(grid, output.astype(bf16))
    grad_norm_two = jnp.einsum("tf,df->td", grad_hidden_b, up_w, preferred_element_type=f32)
    grad_resid = cotan + normal_back(grad_norm_two, scaled_two, inverse_two, gain_two)
    grad_branch_b = grad_resid.astype(bf16)
    proj_far, proj_near = begin_sum(grid, mixed_b, grad_branch_b)
    grad_mixed_b = jnp.einsum(
        "te,de->td", grad_branch_b, proj_w, preferred_element_type=f32
    ).astype(bf16)
    down_got, up_far, proj_far, grad_mixed_b = lax.optimization_barrier(
        (down_got, up_far, proj_far, grad_mixed_b)
    )
    up_got = grid.swap(up_far, Y_BIT)
    down_part = scatter(grid, add_group(down_near, down_got), ("x", "low"))
    probs_b, grad_scores_b = attention_scores_backward(
        query_b, keys_b, values_b, grad_mixed_b, logsum, first_row, key_pos
    )
    up_got, down_part, proj_far, probs_b, grad_scores_b = lax.optimization_barrier(
        (up_got, down_part, proj_far, probs_b, grad_scores_b)
    )
    proj_got = grid.swap(proj_far, Y_BIT)
    up_part = scatter(grid, add_group(up_near, up_got), ("x", "low"))
    down_part = gather(grid, scatter(grid, down_part, ("high",)), ("high", "low"))
    grad_query_b, key_terms, value_terms = attention_products_backward(
        query_b, keys_b, grad_mixed_b, probs_b, grad_scores_b
    )
    proj_got, up_part, down_part, grad_query_b, key_terms, value_terms = (
        lax.optimization_barrier(
            (proj_got, up_part, down_part, grad_query_b, key_terms, value_terms)
        )
    )
    grad_keys_b = (
        key_terms[:tok_rows].astype(f32) + grid.swap(key_terms[tok_rows:], CORE_BIT).astype(f32)
    ).astype(bf16)
    grad_values_b = (
        value_terms[:tok_rows].astype(f32)
        + grid.swap(value_terms[tok_rows:], CORE_BIT).astype(f32)
    ).astype(bf16)
    grad_packed_b = jnp.concatenate([grad_query_b, grad_keys_b, grad_values_b], axis=1)
    packed_far, packed_near = begin_sum(grid, normed_one_b, grad_packed_b)
    packed_got = grid.swap(packed_far, Y_BIT)
    down_part = gather(grid, down_part, ("x", "core"))
    up_part = gather(grid, scatter(grid, up_part, ("high",)), ("high", "low"))
    proj_part = scatter(grid, add_group(proj_near, proj_got), ("x", "low"))
    packed_got, down_part, up_part, proj_part = lax.optimization_barrier(
        (packed_got, down_part, up_part, proj_part)
    )
    grad_down = as_rows(down_part)
    packed_part = scatter(grid, add_group(packed_near, packed_got), ("x", "low", "high"))
    proj_part = scatter(grid, proj_part, ("high",))
    both_columns = jnp.concatenate([packed_part, proj_part], axis=-1)
    both_columns = gather(grid, both_columns, ("high", "low", "x", "core"))
    grad_up = as_rows(gather(grid, up_part, ("x", "core")))
    grad_packed = as_rows(both_columns[..., : 3 * width])
    grad_proj = as_rows(both_columns[..., 3 * width :])
    grad_norm_one = jnp.einsum("te,de->td", grad_packed_b, packed_w, preferred_element_type=f32)
    grad_inputs = grad_resid + normal_back(grad_norm_one, scaled_one, inverse_one, gain_one)
    grad_inputs = jnp.where(
        grid.y == grid.core,
        grad_inputs,
        transpose_pairs(grid, grad_inputs.astype(bf16)).astype(f32),
    )
    sums = (
        jnp.sum(grad_norm_one * scaled_one, axis=0),
        jnp.sum(grad_norm_one, axis=0),
        jnp.sum(grad_query_b.astype(f32), axis=0),
        jnp.sum(grad_values_b.astype(f32), axis=0),
        jnp.sum(grad_branch_b.astype(f32), axis=0),
        jnp.sum(grad_norm_two * scaled_two, axis=0),
        jnp.sum(grad_norm_two, axis=0),
        jnp.sum(grad_hidden_b.astype(f32), axis=0),
        jnp.sum(cotan, axis=0),
    )
    lengths = (width, width, 2 * width, width, width, width, sums[7].shape[0], width)
    totals = summed_everywhere(grid, jnp.concatenate(sums).reshape(-1, 128)).reshape(-1)
    owned, start = [], 0
    for length in lengths:
        owned.append(owned_part(totals[start : start + length], 2))
        start += length
    return (
        output,
        grad_inputs,
        owned[0],
        owned[1],
        grad_packed,
        owned[2],
        grad_proj,
        owned[3],
        owned[4],
        owned[5],
        grad_up,
        owned[6],
        grad_down,
        owned[7],
    )


def solution(mesh):
    two_way = mesh.shape["shard"] == 2 and mesh.shape["rep"] == 16
    return jax.shard_map(
        paired_device if two_way else per_device,
        mesh=mesh,
        in_specs=(
            P(("rep", "shard"), None),
            P("shard"),
            P("shard"),
            P("shard", None),
            P("shard"),
            P("shard", None),
            P("shard"),
            P("shard"),
            P("shard"),
            P("shard", None),
            P("shard"),
            P("shard", None),
            P("shard"),
            P(("rep", "shard"), None),
        ),
        out_specs=(
            P(("rep", "shard"), None),
            P(("rep", "shard"), None),
            P("shard"),
            P("shard"),
            P("shard", None),
            P("shard"),
            P("shard", None),
            P("shard"),
            P("shard"),
            P("shard"),
            P("shard", None),
            P("shard"),
            P("shard", None),
            P("shard"),
        ),
        check_vma=False,
    )
```
